256 devices in a mesh: node: 16 (over y, z_lo, core), local: 16 (over x, z_hi).
Axes of the slice: x: 4, y: 4, z: 8 (z_hi: 4, z_lo: 2; z = z_hi * 2 + z_lo), core: 2. Of those that a mesh axis runs over, the one named last changes fastest.
Arguments:
- inputs: bfloat16 [2048, 8192], P('node', 'local'), may hold values from -21 to 21
- cotangent: bfloat16 [2048, 8192], P('node', 'local'), may hold values from -6 to 6
- gate_codes: bfloat16 [8192, 14336], P('local', 'node'), may hold values from -6 to 6
- gate_blocks: float32 [64, 14336], P('local', 'node'), may hold values from 0.5 to 2
- up_codes: bfloat16 [8192, 14336], P('local', 'node'), may hold values from -12 to 12
- up_blocks: float32 [64, 14336], P('local', 'node'), may hold values from 0.5 to 2
- down_codes: bfloat16 [14336, 8192], P('node', 'local'), may hold values from -6 to 6
- down_blocks: float32 [112, 8192], P('node', 'local'), may hold values from 0.5 to 2
- weight_history: float32 [3, 16], replicated, may hold values from 1 to 5
- grad_history: float32 [3, 16], replicated, may hold values from 512 to 2048
Outputs:
- block_output: bfloat16 [2048, 8192], P('node', 'local')
- grad_gate: bfloat16 [8192, 14336], P('local', 'node')
- grad_up: bfloat16 [8192, 14336], P('local', 'node')
- grad_down: bfloat16 [14336, 8192], P('node', 'local')
- grad_peaks: float32 [3], replicated
The draws below stay inside these ranges and needn't reach their ends.
All inputs are finite; a program needn't handle non-finite values.
Results may differ from the reference program's by a relative error of at most 0.034.
Values may be sent and summed in bfloat16 or wider, within the bound.
No kernel may reach another device: no remote copies, remote signals or barrier semaphores. Data moves between devices by JAX's collectives and lax.ppermute only.
A program may use at most 128 MiB of HBM per device.

```python
import math
import jax
import jax.numpy as jnp
from jax import lax

D = 8192
FF = 14336
QB = 128
HIST = 16
TOKENS = 2048
N_LOCAL = 16


def draw_inputs(key, part):
    key = jax.random.fold_in(key, 11)
    ramp = 3.0 ** (jnp.arange(D, dtype=jnp.float32) / D)
    base = jnp.clip(jax.random.normal(key, (TOKENS, D), jnp.float32), -4.0, 4.0)
    return (base * ramp[None, :]).astype(jnp.bfloat16)


def draw_up_codes(key, part):
    key = jax.random.fold_in(key, 23)
    ramp = 3.0 ** (jnp.arange(FF, dtype=jnp.float32) / FF)
    base = jnp.clip(jax.random.normal(key, (D, FF), jnp.float32), -4.0, 4.0)
    return (base * ramp[None, :]).astype(jnp.bfloat16)


def shard_levels(rng, shape, cuts, smallest, high):
    loudness, own = 1.0, jax.random.fold_in(rng, 6)
    for dim, parts in cuts:
        heights = jnp.exp(jax.random.uniform(jax.random.fold_in(own, dim), (parts,), jnp.float32, smallest / len(cuts), high / len(cuts)))
        loudness = loudness * jnp.repeat(heights, shape[dim] // parts).reshape([-1 if axis == dim else 1 for axis in range(len(shape))])
    return loudness


def normal_values(stream_key, dims, width, reach, pieces=(), kind=jnp.bfloat16):
    level = shard_levels(stream_key, dims, pieces, -0.22, 0.18) if pieces else 1.0
    drawn = jax.random.normal(stream_key, dims, jnp.float32) * width * level
    return jnp.minimum(jnp.maximum(drawn, -reach), reach).astype(kind)


def setup_inputs(seed: int = 0) -> dict:
    seeds = jax.random.split(jax.random.key(seed), 11)
    return {
        "inputs": draw_inputs(jax.random.fold_in(seeds[10], 71), 0),
        "cotangent": normal_values(seeds[1], (TOKENS, D), 1.0, 6.0, ((0, 16), (1, 16))),
        "gate_codes": normal_values(seeds[2], (D, FF), 1.0, 6.0, ((0, 16), (1, 16))),
        "gate_blocks": jnp.clip(jnp.exp(math.log(2.0) - 1.3862944 * jax.random.uniform(seeds[3], (D // QB, FF), jnp.float32) ** shard_levels(seeds[3], (D // QB, FF), ((0, 16), (1, 16)), -0.2, 0.2)), 0.5, 2.0),
        "up_codes": draw_up_codes(jax.random.fold_in(seeds[10], 71), 0),
        "up_blocks": jnp.clip(jnp.exp(math.log(2.0) - 1.3862944 * jax.random.uniform(seeds[5], (D // QB, FF), jnp.float32) ** shard_levels(seeds[5], (D // QB, FF), ((0, 16), (1, 16)), -0.2, 0.2)), 0.5, 2.0),
        "down_codes": normal_values(seeds[6], (FF, D), 1.0, 6.0, ((0, 16), (1, 16))),
        "down_blocks": jnp.clip(jnp.exp(math.log(2.0) - 1.3862944 * jax.random.uniform(seeds[7], (FF // QB, D), jnp.float32) ** shard_levels(seeds[7], (FF // QB, D), ((0, 16), (1, 16)), -0.2, 0.2)), 0.5, 2.0),
        "weight_history": jnp.clip(jnp.exp(jax.random.uniform(seeds[8], (3, HIST), jnp.float32, math.log(1.0), math.log(5.0))), 1.0, 5.0),
        "grad_history": jnp.clip(jnp.exp(jax.random.uniform(seeds[9], (3, HIST), jnp.float32, math.log(512.0), math.log(2048.0))), 512.0, 2048.0),
    }


CODE_LIMIT = 448.0


def dequant(code_values, blocks, tensor_scale):
    row_count, col_count = code_values.shape
    block_count = blocks.shape[0]
    blocked = code_values.astype(jnp.float32).reshape(block_count, row_count // block_count, col_count)
    blocked = blocked * blocks[:, None, :] * tensor_scale
    return blocked.reshape(row_count, col_count).astype(jnp.bfloat16)


def block_sum(left_side, right_side, group_count):
    block_width = left_side.shape[1] // group_count
    running = jnp.zeros((left_side.shape[0], right_side.shape[1]), jnp.float32)
    for group in range(group_count):
        product = jnp.dot(left_side[:, group * block_width:(group + 1) * block_width],
                          right_side[group * block_width:(group + 1) * block_width],
                          preferred_element_type=jnp.float32)
        rounded = lax.optimization_barrier(product.astype(jnp.bfloat16))
        running = running + rounded.astype(jnp.float32)
    return running


def reference(inputs, cotangent, gate_codes, gate_blocks, up_codes, up_blocks, down_codes, down_blocks, weight_history, grad_history):
    scales = jnp.max(weight_history, axis=1) / CODE_LIMIT
    w_gate = dequant(gate_codes, gate_blocks, scales[0])
    w_up = dequant(up_codes, up_blocks, scales[1])
    w_down = dequant(down_codes, down_blocks, scales[2])
    gate_sum = block_sum(inputs, w_gate, N_LOCAL)
    up_sum = block_sum(inputs, w_up, N_LOCAL)
    gate_sig = jax.nn.sigmoid(gate_sum)
    hidden = (gate_sum * gate_sig * up_sum).astype(jnp.bfloat16)
    block_output = jnp.dot(hidden, w_down, preferred_element_type=jnp.float32).astype(jnp.bfloat16)
    back_sum = block_sum(cotangent, w_down.T, N_LOCAL)
    d_gate = (back_sum * up_sum * gate_sig * (1.0 + gate_sum * (1.0 - gate_sig))).astype(jnp.bfloat16)
    d_up = (back_sum * gate_sum * gate_sig).astype(jnp.bfloat16)
    raw_gate = jnp.dot(inputs.T, d_gate, preferred_element_type=jnp.float32)
    raw_up = jnp.dot(inputs.T, d_up, preferred_element_type=jnp.float32)
    raw_down = jnp.dot(hidden.T, cotangent, preferred_element_type=jnp.float32)
    grad_peaks = jnp.stack([jnp.max(jnp.abs(raw_gate)), jnp.max(jnp.abs(raw_up)), jnp.max(jnp.abs(raw_down))])
    grad_max = jnp.max(grad_history, axis=1)
    grad_gate = jnp.clip(raw_gate / grad_max[0], -1.0, 1.0).astype(jnp.bfloat16)
    grad_up = jnp.clip(raw_up / grad_max[1], -1.0, 1.0).astype(jnp.bfloat16)
    grad_down = jnp.clip(raw_down / grad_max[2], -1.0, 1.0).astype(jnp.bfloat16)
    return (block_output, grad_gate, grad_up, grad_down, grad_peaks)
```

```python
import jax
import jax.numpy as jnp
from jax import lax
from jax.experimental import pallas as pl
from jax.experimental.pallas import tpu as pltpu
from jax.sharding import Mesh, PartitionSpec as P

CODE_LIMIT = 448.0
SIZES = {"y": 4, "zl": 2, "c": 2, "x": 4, "zh": 4}
VMEM_LIMIT = 40 * 1024 * 1024
BLOCK = 32
UNITS = (
    (0, ((1, 0), (3, 0), (0, 1), (0, 3))),
    (1, ((3, 0), (1, 0), (0, 3), (0, 1))),
    (3, ((1, 0), (3, 0), (0, 1), (0, 3))),
    (2, ((3, 0), (1, 0), (0, 3), (0, 1))),
)
F32, BF16 = jnp.float32, jnp.bfloat16


def swap(value, mask):
    axis, bits = ("x", mask[0]) if mask[0] else ("zh", mask[1])
    return lax.ppermute(value, axis, [(i, i ^ bits) for i in range(SIZES[axis])])


def shift(value, axis, distance):
    size = SIZES[axis]
    return lax.ppermute(value, axis, [(i, (i + distance) % size) for i in range(size)])


def owners(masks, x, zh):
    order = []
    for t in range(16):
        jx = jz = 0
        for bit, (mx, mz) in enumerate(masks):
            if (t >> (3 - bit)) & 1:
                jx, jz = jx ^ mx, jz ^ mz
        order.append(((x ^ jx) * 4) + (zh ^ jz))
    return jnp.stack(order).astype(jnp.int32)


def params():
    return pltpu.CompilerParams(vmem_limit_bytes=VMEM_LIMIT)


def whole():
    return pl.BlockSpec(memory_space=pltpu.VMEM)


def front_body(perm, a_ref, b_ref, wg_ref, wu_ref, wd_ref, out_ref, rows_ref, all_rows):
    half = a_ref.shape[0]
    all_rows[:half] = a_ref[...]
    all_rows[half:] = b_ref[...]
    for t in range(rows_ref.shape[0] // BLOCK):
        start = pl.multiple_of(perm[t] * BLOCK, BLOCK)
        rows_ref[pl.ds(t * BLOCK, BLOCK), :] = all_rows[pl.ds(start, BLOCK), :]
    depth, width = wg_ref.shape
    x, cot = rows_ref[:, :depth], rows_ref[:, depth:]
    for place, (left, w_ref) in enumerate(((x, wg_ref), (x, wu_ref), (cot, wd_ref))):
        product = jnp.dot(left, w_ref[...], preferred_element_type=F32)
        out_ref[:, place * width:(place + 1) * width] = product.astype(BF16)


def front(perm, a, b, wg, wu, wd_t):
    depth, width = wg.shape
    count = perm.shape[0] * BLOCK
    return pl.pallas_call(
        front_body,
        out_shape=(
            jax.ShapeDtypeStruct((count, 3 * width), BF16),
            jax.ShapeDtypeStruct((count, 2 * depth), BF16),
        ),
        in_specs=[pl.BlockSpec(memory_space=pltpu.SMEM)] + [whole()] * 5,
        out_specs=(whole(), whole()),
        scratch_shapes=[pltpu.VMEM((2 * a.shape[0], a.shape[1]), BF16)],
        compiler_params=params(),
        cost_estimate=pl.CostEstimate(
            flops=6 * count * depth * width, bytes_accessed=9_000_000, transcendentals=0
        ),
        name="front",
    )(perm, a, b, wg, wu, wd_t)


def back_body(perm, lo_ref, hi_ref, w_ref, own_ref, other_ref, all_rows):
    width = w_ref.shape[0]
    half = lo_ref.shape[0]
    for part, ref in enumerate((lo_ref, hi_ref)):
        product = jnp.dot(ref[:, :width], w_ref[...], preferred_element_type=F32).astype(BF16)
        for t in range(half // BLOCK):
            start = pl.multiple_of(perm[part * (half // BLOCK) + t] * BLOCK, BLOCK)
            all_rows[pl.ds(start, BLOCK), :] = product[t * BLOCK:(t + 1) * BLOCK, :]
    own_ref[...] = all_rows[:half]
    other_ref[...] = all_rows[half:]


def back(perm, lo, hi, w_down):
    half, depth = lo.shape[0], w_down.shape[1]
    shape = jax.ShapeDtypeStruct((half, depth), BF16)
    return pl.pallas_call(
        back_body,
        out_shape=(shape, shape),
        in_specs=[pl.BlockSpec(memory_space=pltpu.SMEM)] + [whole()] * 3,
        out_specs=(whole(), whole()),
        scratch_shapes=[pltpu.VMEM((2 * half, depth), BF16)],
        compiler_params=params(),
        cost_estimate=pl.CostEstimate(
            flops=4 * half * depth * w_down.shape[0], bytes_accessed=5_000_000, transcendentals=0
        ),
        name="back",
    )(perm, lo, hi, w_down)


def contract(left, right):
    return lax.dot_general(left, right, (((0,), (0,)), ((), ())), preferred_element_type=F32)


def grads_body(depth, width, *refs):
    acc_in, refs = refs[:3], refs[3:]
    pairs, outs = refs[:-3], refs[-3:]
    sums = [ref[...] for ref in acc_in]
    for rows_ref, acts_ref in zip(pairs[0::2], pairs[1::2]):
        x, cot = rows_ref[:, :depth], rows_ref[:, depth:]
        sums[0] += contract(x, acts_ref[:, width:2 * width])
        sums[1] += contract(x, acts_ref[:, 2 * width:])
        sums[2] += contract(acts_ref[:, :width], cot)
    for ref, total in zip(outs, sums):
        ref[...] = total


def dequant(code_values, blocks, tensor_scale):
    row_count, col_count = code_values.shape
    block_count = blocks.shape[0]
    blocked = code_values.astype(F32).reshape(block_count, row_count // block_count, col_count)
    blocked = blocked * blocks[:, None, :] * tensor_scale
    return blocked.reshape(row_count, col_count).astype(BF16)


def add_halves(keep, received):
    half = keep.shape[0] // 2
    total = keep.astype(F32) + received.astype(F32)
    return total[:half].astype(BF16), total[half:].astype(BF16)


def everywhere_max(value):
    for axis in ("c", "zl", "y", "zh", "x"):
        others = [shift(value, axis, d) for d in range(1, SIZES[axis])]
        for other in others:
            value = jnp.maximum(value, other)
    return value


def shards(
    inputs,
    cotangent,
    gate_codes,
    gate_blocks,
    up_codes,
    up_blocks,
    down_codes,
    down_blocks,
    weight_history,
    grad_history,
):
    x, zh = lax.axis_index("x"), lax.axis_index("zh")
    own = jnp.concatenate([inputs, cotangent], axis=1)
    pair = jnp.concatenate([own, shift(own, "zl", 1)], axis=0)

    scales = jnp.max(weight_history, axis=1) / CODE_LIMIT
    w_gate = dequant(gate_codes, gate_blocks, scales[0])
    w_up = dequant(up_codes, up_blocks, scales[1])
    w_down = dequant(down_codes, down_blocks, scales[2])
    w_down_t = w_down.T
    depth, width = w_gate.shape

    rows, acts, partial_outs = [], [], []
    for distance, masks in UNITS:
        perm = owners(masks, x, zh)
        here = shift(pair, "y", -distance) if distance else pair
        there = shift(here, "c", 1)
        sent, rows_hi = front(perm[8:], here, there, w_gate, w_up, w_down_t)
        received = swap(sent, masks[0])
        keep, rows_lo = front(perm[:8], here, there, w_gate, w_up, w_down_t)
        for mask in masks[1:]:
            keep, sent = add_halves(keep, received)
            received = swap(sent, mask)
        total = keep.astype(F32) + received.astype(F32)
        gate, up, back_sum = jnp.split(total, 3, axis=1)
        sig = jax.nn.sigmoid(gate)
        hidden = gate * sig * up
        d_gate = back_sum * up * sig * (1.0 + gate * (1.0 - sig))
        d_up = back_sum * gate * sig
        held = jnp.concatenate([hidden, d_gate, d_up], axis=1).astype(BF16)
        for mask in masks[:0:-1]:
            held = jnp.concatenate([held, swap(held, mask)], axis=0)
        far = swap(held, masks[0])
        rows.append((rows_lo, rows_hi))
        acts.append((held, far))
        partial_outs.append((distance,) + tuple(back(perm, held, far, w_down)))

    out_total = None
    for distance, mine, other in partial_outs:
        both = mine.astype(F32) + shift(other, "c", 1).astype(F32)
        half = both.shape[0] // 2
        moved = shift(both[half:].astype(BF16), "zl", 1)
        block = both[:half] + moved.astype(F32)
        if distance:
            block = shift(block.astype(BF16), "y", distance).astype(F32)
        out_total = block if out_total is None else out_total + block
    block_output = out_total.astype(BF16)

    raw_gate = raw_up = raw_down = 0.0
    for unit_rows, unit_acts in zip(rows, acts):
        for r, a in zip(unit_rows, unit_acts):
            raw_gate += contract(r[:, :depth], a[:, width:2 * width])
            raw_up += contract(r[:, :depth], a[:, 2 * width:])
            raw_down += contract(a[:, :width], r[:, depth:])
    peak_local = jnp.stack([jnp.max(jnp.abs(r)) for r in (raw_gate, raw_up, raw_down)])
    peak_all = everywhere_max(peak_local)
    grad_max = jnp.max(grad_history, axis=1)
    grad_gate = jnp.clip(raw_gate / grad_max[0], -1.0, 1.0).astype(BF16)
    grad_up = jnp.clip(raw_up / grad_max[1], -1.0, 1.0).astype(BF16)
    grad_down = jnp.clip(raw_down / grad_max[2], -1.0, 1.0).astype(BF16)
    return (block_output, grad_gate, grad_up, grad_down, peak_all)


def solution(mesh):
    names = ("y", "zl", "c", "x", "zh")
    fine = Mesh(mesh.devices.reshape([SIZES[n] for n in names]), names)
    node, local = ("y", "zl", "c"), ("x", "zh")
    acts, weights, weights_t = P(node, local), P(local, node), P(node, local)
    return jax.shard_map(
        shards,
        mesh=fine,
        in_specs=(acts, acts) + (weights,) * 4 + (weights_t,) * 2 + (P(), P()),
        out_specs=(acts, weights, weights, weights_t, P()),
        check_vma=False,
    )
```

```python
import functools

import jax
import jax.numpy as jnp
from jax import lax
from jax.experimental import pallas as pl
from jax.experimental.pallas import tpu as pltpu
from jax.sharding import Mesh, PartitionSpec as P

CODE_LIMIT = 448.0
SIZES = {"y": 4, "zl": 2, "c": 2, "x": 4, "zh": 4}
VMEM_LIMIT = 40 * 1024 * 1024
F32, BF16 = jnp.float32, jnp.bfloat16
CHUNKS = (0, 1, 3, 2)
EARLY = 3
FIRST, SECOND = (1, 3), (3, 1)
ORDER = (
    "F0 F1 F4 F5 A0 A4 F2 B0 F3 B4 C0 A2 C4 D0 F6 D4 F7 G0 G4 A6 B2 E0 B6 E4 C2 J0 C6 D2 J4 D6 G2 G6"
    " E2 E6 K0 J2 J6 K4 K2"
)


def shift(value, axis, distance):
    size = SIZES[axis]
    return lax.ppermute(value, axis, [(i, (i + distance) % size) for i in range(size)])


def meet(value, axis, masks, name):
    pairs = [(c * 4 + i, c * 4 + (i ^ masks[c])) for c in range(2) for i in range(4)]
    with jax.named_scope(name):
        return lax.ppermute(value, ("c", axis), pairs)


class Chain:
    def __init__(self):
        self.last = None

    def __call__(self, body, outs, ins, smem=(), scratch=()):
        extra = [] if self.last is None else [self.last]
        vmem = pl.BlockSpec(memory_space=pltpu.VMEM)
        count_in, count_out = len(smem) + len(ins), len(outs)

        def run(*refs):
            body(*refs[:count_in], *refs[count_in + len(extra):])

        result = pl.pallas_call(
            run,
            out_shape=tuple(jax.ShapeDtypeStruct(*o) for o in outs),
            in_specs=[pl.BlockSpec(memory_space=pltpu.SMEM)] * len(smem)
            + [vmem] * len(ins)
            + [pl.BlockSpec(memory_space=pl.ANY)] * len(extra),
            out_specs=(vmem,) * count_out,
            scratch_shapes=list(scratch),
            compiler_params=pltpu.CompilerParams(vmem_limit_bytes=VMEM_LIMIT),
            cost_estimate=pl.CostEstimate(flops=1, bytes_accessed=1, transcendentals=0),
        )(*smem, *ins, *extra)
        self.last = min(result, key=lambda a: a.size)
        return result


def pack_body(a_ref, b_ref, out_ref):
    width = a_ref.shape[1]
    out_ref[:, :width] = a_ref[...]
    out_ref[:, width:] = b_ref[...]


def stack_body(a_ref, b_ref, out_ref):
    rows = a_ref.shape[0]
    out_ref[:rows] = a_ref[...]
    out_ref[rows:] = b_ref[...]


def weights_body(gc, gb, uc, ub, dc, db, hist, wg_ref, wu_ref, wd_ref, wdt_ref):
    for k, (codes, blocks, out_ref) in enumerate(
        ((gc, gb, wg_ref), (uc, ub, wu_ref), (dc, db, wd_ref))
    ):
        scale = jnp.max(hist[k:k + 1, :], axis=1, keepdims=True) / CODE_LIMIT
        for b in range(blocks.shape[0]):
            part = codes[b * 128:(b + 1) * 128, :].astype(F32) * blocks[b:b + 1, :] * scale
            out_ref[b * 128:(b + 1) * 128, :] = part.astype(BF16)
            if k == 2:
                wdt_ref[:, b * 128:(b + 1) * 128] = part.T.astype(BF16)


def front_body(perm, src_ref, wg_ref, wu_ref, wd_ref, send_ref, keep_ref, rows_ref):
    half = send_ref.shape[0]
    quarter = half // 2
    for t in range(4):
        start = pl.multiple_of(perm[t] * quarter, quarter)
        rows_ref[t * quarter:(t + 1) * quarter, :] = src_ref[pl.ds(start, quarter), :]
    depth, width = wg_ref.shape
    for place, (first, w_ref) in enumerate(((0, wg_ref), (0, wu_ref), (depth, wd_ref))):
        left = rows_ref[:, first:first + depth]
        product = jnp.dot(left, w_ref[...], preferred_element_type=F32).astype(BF16)
        columns = slice(place * width, (place + 1) * width)
        keep_ref[:, columns] = product[:half]
        send_ref[:, columns] = product[half:]


def halve_body(keep_a, keep_b, got_a, got_b, send_ref, left_ref):
    half = keep_a.shape[0] // 2
    for i, (keep, got) in enumerate(((keep_a, got_a), (keep_b, got_b))):
        total = (keep[...].astype(F32) + got[...].astype(F32)).astype(BF16)
        left_ref[i * half:(i + 1) * half] = total[:half]
        send_ref[i * half:(i + 1) * half] = total[half:]


def split_body(perm, keep_ref, got_ref, send_ref, left_ref):
    block = keep_ref.shape[0] // 4
    for t in range(4):
        rows = pl.ds(pl.multiple_of(perm[t] * block, block), block)
        total = (keep_ref[rows, :].astype(F32) + got_ref[rows, :].astype(F32)).astype(BF16)
        ref = left_ref if t < 2 else send_ref
        ref[(t % 2) * block:(t % 2 + 1) * block] = total


def quarter_body(keep_ref, got_ref, send_ref, left_ref):
    block = keep_ref.shape[0] // 2
    total = (keep_ref[...].astype(F32) + got_ref[...].astype(F32)).astype(BF16)
    left_ref[...] = total[:block]
    send_ref[...] = total[block:]


def middle_body(keep_ref, got_ref, out_ref):
    total = keep_ref[...].astype(F32) + got_ref[...].astype(F32)
    width = total.shape[1] // 3
    gate, up, back = total[:, :width], total[:, width:2 * width], total[:, 2 * width:]
    sig = jax.nn.sigmoid(gate)
    out_ref[:, :width] = (gate * sig * up).astype(BF16)
    out_ref[:, width:2 * width] = (back * up * sig * (1.0 + gate * (1.0 - sig))).astype(BF16)
    out_ref[:, 2 * width:] = (back * gate * sig).astype(BF16)


def unsplit_body(perm, near_ref, far_ref, out_ref):
    block = near_ref.shape[0] // 2
    for t in range(4):
        ref = near_ref if t < 2 else far_ref
        rows = pl.ds(pl.multiple_of(perm[t] * block, block), block)
        out_ref[rows, :] = ref[(t % 2) * block:(t % 2 + 1) * block]


def unhalve_body(own_ref, got_ref, out_ref):
    half = own_ref.shape[0] // 2
    for i in range(2):
        out_ref[2 * i * half:(2 * i + 1) * half] = own_ref[i * half:(i + 1) * half]
        out_ref[(2 * i + 1) * half:(2 * i + 2) * half] = got_ref[i * half:(i + 1) * half]


def back_body(perm, near_ref, far_ref, w_ref, own_ref, other_ref):
    width = w_ref.shape[0]
    half = near_ref.shape[0] // 2
    for part, ref in enumerate((near_ref, far_ref)):
        product = jnp.dot(ref[:, :width], w_ref[...], preferred_element_type=F32).astype(BF16)
        quarter = half // 2
        for i, out_ref in enumerate((own_ref, other_ref)):
            for t in range(2):
                start = pl.multiple_of(perm[2 * part + t] * quarter, quarter)
                place = i * half + t * quarter
                out_ref[pl.ds(start, quarter), :] = product[place:place + quarter]


def pile_body(*refs):
    place = 0
    for ref in refs[:-1]:
        refs[-1][place:place + ref.shape[0]] = ref[...]
        place += ref.shape[0]


def cores_body(got_ref, *refs):
    mine, (keep_ref, send_ref) = refs[:-2], refs[-2:]
    rows = mine[0].shape[0]
    half = rows // 2
    for i, ref in enumerate(mine):
        total = ref[...].astype(F32) + got_ref[i * rows:(i + 1) * rows].astype(F32)
        keep_ref[i * half:(i + 1) * half] = total[:half].astype(BF16)
        send_ref[i * half:(i + 1) * half] = total[half:].astype(BF16)


def pairs_body(keep_ref, got_ref, *outs):
    total = keep_ref[...].astype(F32) + got_ref[...].astype(F32)
    rows = outs[0].shape[0]
    for i, ref in enumerate(outs):
        ref[...] = total[i * rows:(i + 1) * rows].astype(BF16)


def total_body(*refs):
    total = refs[0][...].astype(F32)
    for ref in refs[1:-1]:
        total += ref[...].astype(F32)
    refs[-1][...] = total.astype(BF16)


def max_body(a_ref, b_ref, out_ref):
    out_ref[...] = jnp.maximum(a_ref[...], b_ref[...])


def contract(left, right):
    return lax.dot_general(left, right, (((0,), (0,)), ((), ())), preferred_element_type=F32)


def gather_rows(refs, columns, scratch):
    place = 0
    for ref in refs:
        scratch[place:place + ref.shape[0], :] = ref[:, columns]
        place += ref.shape[0]
    return scratch[...]


def gather_acts(refs, columns, scratch):
    place = 0
    for near, far in zip(refs[0::2], refs[1::2]):
        half = near.shape[0] // 2
        for i in range(2):
            for ref in (near, far):
                scratch[place:place + half, :] = ref[i * half:(i + 1) * half, columns]
                place += half
    return scratch[...]


def grad_body(which, depth, width, count, *refs):
    rows, acts, out_ref, left, right = refs[:count], refs[count:-3], refs[-3], refs[-2], refs[-1]
    places = [slice(width, 2 * width), slice(2 * width, 3 * width), slice(0, width)]
    first = slice(depth, 2 * depth) if which == 2 else slice(0, depth)
    r, a = gather_rows(rows, first, left), gather_acts(acts, places[which], right)
    out_ref[...] = contract(a, r) if which == 2 else contract(r, a)


def last_body(depth, width, count, hist, *refs):
    rows, refs = refs[:count], refs[count:]
    acts, totals, outs, peak_ref = refs[:count], refs[count:count + 3], refs[-6:-3], refs[-3]
    left, right = refs[-2:]
    places = [slice(width, 2 * width), slice(2 * width, 3 * width), slice(0, width)]
    x = gather_rows(rows, slice(0, depth), left)
    peak_ref[...] = jnp.zeros_like(peak_ref)
    for which in (0, 1, 2):
        if which == 2:
            x = gather_rows(rows, slice(depth, 2 * depth), left)
        a = gather_acts(acts, places[which], right)
        total = totals[which][...] + (contract(a, x) if which == 2 else contract(x, a))
        peak = jnp.max(jnp.max(jnp.abs(total), axis=0, keepdims=True), axis=1, keepdims=True)
        peak_ref[which:which + 1, :] = jnp.broadcast_to(peak, (1, peak_ref.shape[1]))
        scale = jnp.max(hist[which:which + 1, :], axis=1, keepdims=True)
        outs[which][...] = jnp.clip(total / scale, -1.0, 1.0).astype(BF16)


def shards(
    inputs,
    cotangent,
    gate_codes,
    gate_blocks,
    up_codes,
    up_blocks,
    down_codes,
    down_blocks,
    weight_history,
    grad_history,
):
    core, x, zh = lax.axis_index("c"), lax.axis_index("x"), lax.axis_index("zh")
    first = jnp.where(core == 0, FIRST[0], FIRST[1])
    second = jnp.where(core == 0, SECOND[0], SECOND[1])
    perm_mine = jnp.stack([x, x ^ second, x ^ first, x ^ first ^ second]).astype(jnp.int32)
    perm_other = jnp.array([0, 2, 1, 3], jnp.int32)
    perm_z = jnp.stack([zh, zh ^ second, zh ^ first, zh ^ first ^ second]).astype(jnp.int32)
    perm_same = jnp.arange(4, dtype=jnp.int32)
    depth, width = gate_codes.shape
    tokens = inputs.shape[0]
    rows_in_unit, half, quarter = 2 * tokens, tokens, tokens // 2

    call = Chain()
    (own,) = call(pack_body, [((tokens, 2 * depth), BF16)], [inputs, cotangent])
    own_zl = shift(own, "zl", 1)
    wg, wu, wd, wd_t = call(
        weights_body,
        [((depth, width), BF16), ((depth, width), BF16), ((width, depth), BF16), ((depth, width), BF16)],
        [gate_codes, gate_blocks, up_codes, up_blocks, down_codes, down_blocks, weight_history],
    )
    (pair,) = call(stack_body, [((rows_in_unit, 2 * depth), BF16)], [own, own_zl])
    here = {0: pair, 1: shift(pair, "y", -1), 3: shift(pair, "y", 1)}

    rows, keep, got, held, far, there, outs = {}, {}, {}, {}, {}, {}, {}
    wide = 3 * width
    chunk_rows = 2 * rows_in_unit

    def front(u):
        distance, mine = CHUNKS[u // 2], u % 2 == 0
        perm = (perm_same if distance == 2 else perm_mine) if mine else perm_other
        sent, keep[u], rows[u] = call(
            front_body,
            [((half, wide), BF16)] * 2 + [((rows_in_unit, 2 * depth), BF16)],
            [here[distance] if mine else there[distance], wg, wu, wd_t],
            smem=[perm],
        )
        got[u] = meet(sent, "x", FIRST, f"halves_{u}")
        if mine:
            with jax.named_scope(f"rows_{u}"):
                there[distance] = shift(rows[u], "c", 1)
        if distance == 1 and mine:
            with jax.named_scope("rows_far"):
                here[2] = shift(rows[u], "y", -1)

    def reduce_step(kind, u):
        if kind == "A":
            sent, keep[u] = call(
                halve_body,
                [((half, wide), BF16)] * 2,
                [keep[u], keep[u + 1], got[u], got[u + 1]],
            )
            got[u] = meet(sent, "x", SECOND, f"quarters_{u}")
        elif kind == "B":
            shapes = [((quarter, wide), BF16)] * 2
            sent, keep[u] = call(split_body, shapes, [keep[u], got[u]], smem=[perm_z])
            got[u] = meet(sent, "zh", FIRST, f"eighths_{u}")
        elif kind == "C":
            shapes = [((quarter // 2, wide), BF16)] * 2
            sent, keep[u] = call(quarter_body, shapes, [keep[u], got[u]])
            got[u] = meet(sent, "zh", SECOND, f"sixteenths_{u}")
        else:
            (keep[u],) = call(middle_body, [((quarter // 2, wide), BF16)], [keep[u], got[u]])
            got[u] = meet(keep[u], "zh", SECOND, f"back_sixteenths_{u}")

    def gather_step(kind, u):
        if kind == "G":
            (keep[u],) = call(pile_body, [((quarter, wide), BF16)], [keep[u], got[u]])
            got[u] = meet(keep[u], "zh", FIRST, f"back_eighths_{u}")
        elif kind == "E":
            shapes = [((half, wide), BF16)]
            (keep[u],) = call(unsplit_body, shapes, [keep[u], got[u]], smem=[perm_z])
            got[u] = meet(keep[u], "x", SECOND, f"back_quarters_{u}")
        else:
            (held[u],) = call(unhalve_body, [((rows_in_unit, wide), BF16)], [keep[u], got[u]])
            far[u] = meet(held[u], "x", FIRST, f"back_halves_{u}")

    def finish(u):
        shapes = [((rows_in_unit, depth), BF16)] * 2
        outs[u], outs[u + 1] = call(back_body, shapes, [held[u], far[u], wd], smem=[perm_mine])

    for step in ORDER.split():
        kind, u = step[0], int(step[1:])
        if kind == "F":
            front(u)
        elif kind in "ABCD":
            reduce_step(kind, u)
        elif kind in "GEJ":
            gather_step(kind, u)
        else:
            finish(u)

    def send_cores(chunks):
        other = [outs[2 * p + 1] for p in chunks]
        if len(other) > 1:
            other = call(pile_body, [((len(other) * rows_in_unit, depth), BF16)], other)
        return shift(other[0], "c", 1), [outs[2 * p] for p in chunks], [CHUNKS[p] for p in chunks]

    def send_pairs(came, mine):
        left, sent = call(cores_body, [((len(mine) * half, depth), BF16)] * 2, [came] + mine)
        return left, shift(sent, "zl", 1)

    def send_home(left, came, distances):
        blocks = call(pairs_body, [((half, depth), BF16)] * len(distances), [left, came])
        return [shift(b, "y", d) if d else b for b, d in zip(blocks, distances)]

    early, late = range(EARLY), range(EARLY, len(CHUNKS))
    came, mine, distances = send_cores(early)
    early_rows = [rows[u] for p in early for u in (2 * p, 2 * p + 1)]
    early_acts = [part for p in early for part in (held[2 * p], far[2 * p])]
    totals = []
    for which in range(3):
        (total,) = call(
            functools.partial(grad_body, which, depth, width, len(early_rows)),
            [((width, depth) if which == 2 else (depth, width), F32)],
            early_rows + early_acts,
            scratch=[
                pltpu.VMEM((EARLY * chunk_rows, depth), BF16),
                pltpu.VMEM((EARLY * chunk_rows, width), BF16),
            ],
        )
        totals.append(total)
        if which == 0:
            left, came = send_pairs(came, mine)
    blocks = send_home(left, came, distances)
    for p in late:
        finish(2 * p)
    came, mine, distances = send_cores(late)
    late_rows = [rows[u] for p in late for u in (2 * p, 2 * p + 1)]
    grad_gate, grad_up, grad_down, peaks = call(
        functools.partial(last_body, depth, width, len(late_rows)),
        [((depth, width), BF16), ((depth, width), BF16), ((width, depth), BF16), ((8, 128), F32)],
        [grad_history] + late_rows + [part for p in late for part in (held[2 * p], far[2 * p])] + totals,
        scratch=[
            pltpu.VMEM((len(late) * chunk_rows, depth), BF16),
            pltpu.VMEM((len(late) * chunk_rows, width), BF16),
        ],
    )
    steps = [("c", 1), ("zl", 1), ("y", 1), ("y", 3), ("zh", 1), ("zh", 3), ("x", 1), ("x", 3)]
    for i, (axis, mask) in enumerate(steps):
        size = SIZES[axis]
        seen = lax.ppermute(peaks, axis, [(j, j ^ mask) for j in range(size)])
        if i == 0:
            left, came = send_pairs(came, mine)
        elif i == 1:
            blocks += send_home(left, came, distances)
        elif i == 5:
            (block_output,) = call(total_body, [((half, depth), BF16)], blocks)
        (peaks,) = call(max_body, [((8, 128), F32)], [peaks, seen])
    peak_all = peaks[:3, 0]
    return (block_output, grad_gate, grad_up, grad_down, peak_all)


def solution(mesh):
    names = ("y", "zl", "c", "x", "zh")
    fine = Mesh(mesh.devices.reshape([SIZES[n] for n in names]), names)
    node, local = ("y", "zl", "c"), ("x", "zh")
    acts, weights, weights_t = P(node, local), P(local, node), P(node, local)
    return jax.shard_map(
        shards,
        mesh=fine,
        in_specs=(acts, acts) + (weights,) * 4 + (weights_t,) * 2 + (P(), P()),
        out_specs=(acts, weights, weights, weights_t, P()),
        check_vma=False,
    )
```

```python
import functools

import jax
import jax.numpy as jnp
from jax import lax
from jax.experimental import pallas as pl
from jax.experimental.pallas import tpu as pltpu
from jax.sharding import Mesh, PartitionSpec as P

CODE_LIMIT = 448.0
SIZES = {"y": 4, "zl": 2, "c": 2, "x": 4, "zh": 4}
VMEM_LIMIT = 40 * 1024 * 1024
F32, BF16 = jnp.float32, jnp.bfloat16
CHUNKS = (0, 1, 3, 2)
MODES = "mmmm"
EARLY = 3
FIRST, SECOND = (1, 3), (3, 1)
ORDER = (
    "F0 F1 A0 F4", "F2 F3 B0 A2", "C0 F5 B2 A4", "F6 E0 B4 C2", "F7 J0 C4 A6",
    "E2 B6 E4 J2", "C6 J4 K0 E6", "K2 K4 J6",
)


def shift(value, axis, distance):
    size = SIZES[axis]
    return lax.ppermute(value, axis, [(i, (i + distance) % size) for i in range(size)])


def meet(value, axis, masks, name):
    pairs = [(c * 4 + i, c * 4 + (i ^ masks[c])) for c in range(2) for i in range(4)]
    with jax.named_scope(name):
        return lax.ppermute(value, ("c", axis), pairs)


class Chain:
    def __init__(self):
        self.last = None

    def __call__(self, body, outs, ins, smem=(), scratch=()):
        extra = [] if self.last is None else [self.last]
        vmem = pl.BlockSpec(memory_space=pltpu.VMEM)
        count_in, count_out = len(smem) + len(ins), len(outs)

        def run(*refs):
            body(*refs[:count_in], *refs[count_in + len(extra):])

        result = pl.pallas_call(
            run,
            out_shape=tuple(jax.ShapeDtypeStruct(*o) for o in outs),
            in_specs=[pl.BlockSpec(memory_space=pltpu.SMEM)] * len(smem)
            + [vmem] * len(ins)
            + [pl.BlockSpec(memory_space=pl.ANY)] * len(extra),
            out_specs=(vmem,) * count_out,
            scratch_shapes=list(scratch),
            compiler_params=pltpu.CompilerParams(vmem_limit_bytes=VMEM_LIMIT),
            cost_estimate=pl.CostEstimate(flops=1, bytes_accessed=1, transcendentals=0),
        )(*smem, *ins, *extra)
        self.last = min(result, key=lambda a: a.size)
        return result


def pack_body(a_ref, b_ref, out_ref):
    width = a_ref.shape[1]
    out_ref[:, :width] = a_ref[...]
    out_ref[:, width:] = b_ref[...]


def stack_body(a_ref, b_ref, out_ref):
    rows = a_ref.shape[0]
    out_ref[:rows] = a_ref[...]
    out_ref[rows:] = b_ref[...]


def weights_body(gc, gb, uc, ub, dc, db, hist, wg_ref, wu_ref, wd_ref, wdt_ref):
    for k, (codes, blocks, out_ref) in enumerate(
        ((gc, gb, wg_ref), (uc, ub, wu_ref), (dc, db, wd_ref))
    ):
        scale = jnp.max(hist[k:k + 1, :], axis=1, keepdims=True) / CODE_LIMIT
        for b in range(blocks.shape[0]):
            part = codes[b * 128:(b + 1) * 128, :].astype(F32) * blocks[b:b + 1, :] * scale
            out_ref[b * 128:(b + 1) * 128, :] = part.astype(BF16)
            if k == 2:
                wdt_ref[:, b * 128:(b + 1) * 128] = part.T.astype(BF16)


def front_body(perm, src_ref, wg_ref, wu_ref, wd_ref, send_ref, keep_ref, rows_ref):
    half = send_ref.shape[0]
    quarter = half // 2
    for t in range(4):
        start = pl.multiple_of(perm[t] * quarter, quarter)
        rows_ref[t * quarter:(t + 1) * quarter, :] = src_ref[pl.ds(start, quarter), :]
    depth, width = wg_ref.shape
    for place, (first, w_ref) in enumerate(((0, wg_ref), (0, wu_ref), (depth, wd_ref))):
        left = rows_ref[:, first:first + depth]
        product = jnp.dot(left, w_ref[...], preferred_element_type=F32).astype(BF16)
        columns = slice(place * width, (place + 1) * width)
        keep_ref[:, columns] = product[:half]
        send_ref[:, columns] = product[half:]


def halve_body(keep_a, keep_b, got_a, got_b, send_ref, left_ref):
    half = keep_a.shape[0] // 2
    for i, (keep, got) in enumerate(((keep_a, got_a), (keep_b, got_b))):
        total = (keep[...].astype(F32) + got[...].astype(F32)).astype(BF16)
        left_ref[i * half:(i + 1) * half] = total[:half]
        send_ref[i * half:(i + 1) * half] = total[half:]


def split_body(perm, keep_ref, got_ref, send_ref, left_ref):
    block = keep_ref.shape[0] // 4
    for t in range(4):
        rows = pl.ds(pl.multiple_of(perm[t] * block, block), block)
        total = (keep_ref[rows, :].astype(F32) + got_ref[rows, :].astype(F32)).astype(BF16)
        ref = left_ref if t < 2 else send_ref
        ref[(t % 2) * block:(t % 2 + 1) * block] = total


def add_body(keep_ref, got_ref, out_ref):
    out_ref[...] = (keep_ref[...].astype(F32) + got_ref[...].astype(F32)).astype(BF16)


def quarter_body(keep_ref, got_ref, send_ref, left_ref):
    block = keep_ref.shape[0] // 2
    total = (keep_ref[...].astype(F32) + got_ref[...].astype(F32)).astype(BF16)
    left_ref[...] = total[:block]
    send_ref[...] = total[block:]


def middle_body(keep_ref, got_ref, out_ref):
    total = keep_ref[...].astype(F32) + got_ref[...].astype(F32)
    width = total.shape[1] // 3
    gate, up, back = total[:, :width], total[:, width:2 * width], total[:, 2 * width:]
    sig = jax.nn.sigmoid(gate)
    out_ref[:, :width] = (gate * sig * up).astype(BF16)
    out_ref[:, width:2 * width] = (back * up * sig * (1.0 + gate * (1.0 - sig))).astype(BF16)
    out_ref[:, 2 * width:] = (back * gate * sig).astype(BF16)


def unsplit_body(perm, near_ref, far_ref, out_ref):
    block = near_ref.shape[0] // 2
    for t in range(4):
        ref = near_ref if t < 2 else far_ref
        rows = pl.ds(pl.multiple_of(perm[t] * block, block), block)
        out_ref[rows, :] = ref[(t % 2) * block:(t % 2 + 1) * block]


def unhalve_body(own_ref, got_ref, out_ref):
    half = own_ref.shape[0] // 2
    for i in range(2):
        out_ref[2 * i * half:(2 * i + 1) * half] = own_ref[i * half:(i + 1) * half]
        out_ref[(2 * i + 1) * half:(2 * i + 2) * half] = got_ref[i * half:(i + 1) * half]


def back_body(perm, near_ref, far_ref, w_ref, own_ref, other_ref):
    width = w_ref.shape[0]
    half = near_ref.shape[0] // 2
    for part, ref in enumerate((near_ref, far_ref)):
        product = jnp.dot(ref[:, :width], w_ref[...], preferred_element_type=F32).astype(BF16)
        quarter = half // 2
        for i, out_ref in enumerate((own_ref, other_ref)):
            for t in range(2):
                start = pl.multiple_of(perm[2 * part + t] * quarter, quarter)
                place = i * half + t * quarter
                out_ref[pl.ds(start, quarter), :] = product[place:place + quarter]


def pile_body(*refs):
    place = 0
    for ref in refs[:-1]:
        refs[-1][place:place + ref.shape[0]] = ref[...]
        place += ref.shape[0]


def cores_body(got_ref, *refs):
    mine, (keep_ref, send_ref) = refs[:-2], refs[-2:]
    rows = mine[0].shape[0]
    half = rows // 2
    for i, ref in enumerate(mine):
        total = ref[...].astype(F32) + got_ref[i * rows:(i + 1) * rows].astype(F32)
        keep_ref[i * half:(i + 1) * half] = total[:half].astype(BF16)
        send_ref[i * half:(i + 1) * half] = total[half:].astype(BF16)


def pairs_body(keep_ref, got_ref, *outs):
    total = keep_ref[...].astype(F32) + got_ref[...].astype(F32)
    rows = outs[0].shape[0]
    for i, ref in enumerate(outs):
        ref[...] = total[i * rows:(i + 1) * rows].astype(BF16)


def total_body(*refs):
    total = refs[0][...].astype(F32)
    for ref in refs[1:-1]:
        total += ref[...].astype(F32)
    refs[-1][...] = total.astype(BF16)


def max_body(a_ref, b_ref, out_ref):
    out_ref[...] = jnp.maximum(a_ref[...], b_ref[...])


def contract(left, right):
    return lax.dot_general(left, right, (((0,), (0,)), ((), ())), preferred_element_type=F32)


def gather_rows(refs, columns, scratch):
    place = 0
    for ref in refs:
        scratch[place:place + ref.shape[0], :] = ref[:, columns]
        place += ref.shape[0]
    return scratch[...]


def gather_acts(refs, columns, scratch):
    place = 0
    for near, far in zip(refs[0::2], refs[1::2]):
        half = near.shape[0] // 2
        for i in range(2):
            for ref in (near, far):
                scratch[place:place + half, :] = ref[i * half:(i + 1) * half, columns]
                place += half
    return scratch[...]


def grad_body(which, depth, width, count, *refs):
    rows, acts, out_ref, left, right = refs[:count], refs[count:-3], refs[-3], refs[-2], refs[-1]
    places = [slice(width, 2 * width), slice(2 * width, 3 * width), slice(0, width)]
    first = slice(depth, 2 * depth) if which == 2 else slice(0, depth)
    r, a = gather_rows(rows, first, left), gather_acts(acts, places[which], right)
    out_ref[...] = contract(a, r) if which == 2 else contract(r, a)


def last_body(depth, width, count, hist, *refs):
    rows, refs = refs[:count], refs[count:]
    acts, totals, outs, peak_ref = refs[:count], refs[count:count + 3], refs[-6:-3], refs[-3]
    left, right = refs[-2:]
    places = [slice(width, 2 * width), slice(2 * width, 3 * width), slice(0, width)]
    x = gather_rows(rows, slice(0, depth), left)
    peak_ref[...] = jnp.zeros_like(peak_ref)
    for which in (0, 1, 2):
        if which == 2:
            x = gather_rows(rows, slice(depth, 2 * depth), left)
        a = gather_acts(acts, places[which], right)
        total = totals[which][...] + (contract(a, x) if which == 2 else contract(x, a))
        peak = jnp.max(jnp.max(jnp.abs(total), axis=0, keepdims=True), axis=1, keepdims=True)
        peak_ref[which:which + 1, :] = jnp.broadcast_to(peak, (1, peak_ref.shape[1]))
        scale = jnp.max(hist[which:which + 1, :], axis=1, keepdims=True)
        outs[which][...] = jnp.clip(total / scale, -1.0, 1.0).astype(BF16)


def shards(
    inputs,
    cotangent,
    gate_codes,
    gate_blocks,
    up_codes,
    up_blocks,
    down_codes,
    down_blocks,
    weight_history,
    grad_history,
):
    core, x, zh = lax.axis_index("c"), lax.axis_index("x"), lax.axis_index("zh")
    first = jnp.where(core == 0, FIRST[0], FIRST[1])
    second = jnp.where(core == 0, SECOND[0], SECOND[1])
    perm_mine = jnp.stack([x, x ^ second, x ^ first, x ^ first ^ second]).astype(jnp.int32)
    perm_other = jnp.array([0, 2, 1, 3], jnp.int32)
    perm_z = jnp.stack([zh, zh ^ second, zh ^ first, zh ^ first ^ second]).astype(jnp.int32)
    perm_same = jnp.arange(4, dtype=jnp.int32)
    depth, width = gate_codes.shape
    tokens = inputs.shape[0]
    rows_in_unit, half, quarter = 2 * tokens, tokens, tokens // 2

    call = Chain()
    (own,) = call(pack_body, [((tokens, 2 * depth), BF16)], [inputs, cotangent])
    own_zl = shift(own, "zl", 1)
    wg, wu, wd, wd_t = call(
        weights_body,
        [((depth, width), BF16), ((depth, width), BF16), ((width, depth), BF16), ((depth, width), BF16)],
        [gate_codes, gate_blocks, up_codes, up_blocks, down_codes, down_blocks, weight_history],
    )
    (pair,) = call(stack_body, [((rows_in_unit, 2 * depth), BF16)], [own, own_zl])
    here = {0: pair, 1: shift(pair, "y", -1), 3: shift(pair, "y", 1)}

    rows, keep, got, held, far, there, outs = {}, {}, {}, {}, {}, {}, {}
    wide = 3 * width
    chunk_rows = 2 * rows_in_unit

    def front(u):
        distance, mine = CHUNKS[u // 2], u % 2 == 0
        perm = (perm_same if distance == 2 else perm_mine) if mine else perm_other
        sent, keep[u], rows[u] = call(
            front_body,
            [((half, wide), BF16)] * 2 + [((rows_in_unit, 2 * depth), BF16)],
            [here[distance] if mine else there[distance], wg, wu, wd_t],
            smem=[perm],
        )
        got[u] = meet(sent, "x", FIRST, f"halves_{u}")
        if mine:
            with jax.named_scope(f"rows_{u}"):
                there[distance] = shift(rows[u], "c", 1)
        if distance == 1 and mine:
            with jax.named_scope("rows_far"):
                here[2] = shift(rows[u], "y", -1)

    def reduce_step(kind, u):
        if kind == "A":
            sent, keep[u] = call(
                halve_body,
                [((half, wide), BF16)] * 2,
                [keep[u], keep[u + 1], got[u], got[u + 1]],
            )
            got[u] = meet(sent, "x", SECOND, f"quarters_{u}")
        elif MODES[u // 2] == "m":
            (keep[u],) = call(add_body, [((half, wide), BF16)], [keep[u], got[u]])
            masks, name = (FIRST, "first") if kind == "B" else (SECOND, "second")
            got[u] = meet(keep[u], "zh", masks, f"rows_{name}_{u}")
        elif kind == "B":
            shapes = [((quarter, wide), BF16)] * 2
            sent, keep[u] = call(split_body, shapes, [keep[u], got[u]], smem=[perm_z])
            got[u] = meet(sent, "zh", FIRST, f"eighths_{u}")
        elif kind == "C":
            shapes = [((quarter // 2, wide), BF16)] * 2
            sent, keep[u] = call(quarter_body, shapes, [keep[u], got[u]])
            got[u] = meet(sent, "zh", SECOND, f"sixteenths_{u}")
        else:
            (keep[u],) = call(middle_body, [((quarter // 2, wide), BF16)], [keep[u], got[u]])
            got[u] = meet(keep[u], "zh", SECOND, f"back_sixteenths_{u}")

    def gather_step(kind, u):
        if kind == "G":
            (keep[u],) = call(pile_body, [((quarter, wide), BF16)], [keep[u], got[u]])
            got[u] = meet(keep[u], "zh", FIRST, f"back_eighths_{u}")
        elif kind == "E":
            shapes = [((half, wide), BF16)]
            if MODES[u // 2] == "m":
                (keep[u],) = call(middle_body, shapes, [keep[u], got[u]])
            else:
                (keep[u],) = call(unsplit_body, shapes, [keep[u], got[u]], smem=[perm_z])
            got[u] = meet(keep[u], "x", SECOND, f"back_quarters_{u}")
        else:
            (held[u],) = call(unhalve_body, [((rows_in_unit, wide), BF16)], [keep[u], got[u]])
            far[u] = meet(held[u], "x", FIRST, f"back_halves_{u}")

    def finish(u):
        shapes = [((rows_in_unit, depth), BF16)] * 2
        outs[u], outs[u + 1] = call(back_body, shapes, [held[u], far[u], wd], smem=[perm_mine])

    for step in " ".join(ORDER).split():
        kind, u = step[0], int(step[1:])
        if kind == "F":
            front(u)
        elif kind in "ABCD":
            reduce_step(kind, u)
        elif kind in "GEJ":
            gather_step(kind, u)
        else:
            finish(u)

    def send_cores(chunks):
        other = [outs[2 * p + 1] for p in chunks]
        if len(other) > 1:
            other = call(pile_body, [((len(other) * rows_in_unit, depth), BF16)], other)
        return shift(other[0], "c", 1), [outs[2 * p] for p in chunks], [CHUNKS[p] for p in chunks]

    def send_pairs(came, mine):
        left, sent = call(cores_body, [((len(mine) * half, depth), BF16)] * 2, [came] + mine)
        return left, shift(sent, "zl", 1)

    def send_home(left, came, distances):
        blocks = call(pairs_body, [((half, depth), BF16)] * len(distances), [left, came])
        return [shift(b, "y", d) if d else b for b, d in zip(blocks, distances)]

    early, late = range(EARLY), range(EARLY, len(CHUNKS))
    came, mine, distances = send_cores(early)
    early_rows = [rows[u] for p in early for u in (2 * p, 2 * p + 1)]
    early_acts = [part for p in early for part in (held[2 * p], far[2 * p])]
    totals = []
    for which in range(3):
        (total,) = call(
            functools.partial(grad_body, which, depth, width, len(early_rows)),
            [((width, depth) if which == 2 else (depth, width), F32)],
            early_rows + early_acts,
            scratch=[
                pltpu.VMEM((EARLY * chunk_rows, depth), BF16),
                pltpu.VMEM((EARLY * chunk_rows, width), BF16),
            ],
        )
        totals.append(total)
        if which == 0:
            left, came = send_pairs(came, mine)
    blocks = send_home(left, came, distances)
    for p in late:
        finish(2 * p)
    came, mine, distances = send_cores(late)
    late_rows = [rows[u] for p in late for u in (2 * p, 2 * p + 1)]
    grad_gate, grad_up, grad_down, peaks = call(
        functools.partial(last_body, depth, width, len(late_rows)),
        [((depth, width), BF16), ((depth, width), BF16), ((width, depth), BF16), ((8, 128), F32)],
        [grad_history] + late_rows + [part for p in late for part in (held[2 * p], far[2 * p])] + totals,
        scratch=[
            pltpu.VMEM((len(late) * chunk_rows, depth), BF16),
            pltpu.VMEM((len(late) * chunk_rows, width), BF16),
        ],
    )
    steps = [("c", 1), ("zl", 1), ("y", 1), ("y", 3), ("zh", 1), ("zh", 3), ("x", 1), ("x", 3)]
    for i, (axis, mask) in enumerate(steps):
        size = SIZES[axis]
        seen = lax.ppermute(peaks, axis, [(j, j ^ mask) for j in range(size)])
        if i == 0:
            left, came = send_pairs(came, mine)
        elif i == 1:
            blocks += send_home(left, came, distances)
        elif i == 5:
            (block_output,) = call(total_body, [((half, depth), BF16)], blocks)
        (peaks,) = call(max_body, [((8, 128), F32)], [peaks, seen])
    peak_all = peaks[:3, 0]
    return (block_output, grad_gate, grad_up, grad_down, peak_all)


def solution(mesh):
    names = ("y", "zl", "c", "x", "zh")
    fine = Mesh(mesh.devices.reshape([SIZES[n] for n in names]), names)
    node, local = ("y", "zl", "c"), ("x", "zh")
    acts, weights, weights_t = P(node, local), P(local, node), P(node, local)
    return jax.shard_map(
        shards,
        mesh=fine,
        in_specs=(acts, acts) + (weights,) * 4 + (weights_t,) * 2 + (P(), P()),
        out_specs=(acts, weights, weights, weights_t, P()),
        check_vma=False,
    )
```

```python
import functools

import jax
import jax.numpy as jnp
from jax import lax
from jax.experimental import pallas as pl
from jax.experimental.pallas import tpu as pltpu
from jax.sharding import Mesh, PartitionSpec as P

CODE_LIMIT = 448.0
SIZES = {"y": 4, "zl": 2, "c": 2, "x": 4, "zh": 4}
VMEM_LIMIT = 40 * 1024 * 1024
F32, BF16 = jnp.float32, jnp.bfloat16
CHUNKS = (0, 1, 3, 2)
MODES = "mmmm"
EARLY = 3
FIRST, SECOND = (1, 3), (3, 1)
ORDER = (
    "F0 F1 A0 F4", "F2 F3 B0 A2", "F5 C0 B2 A4", "E0 F6 B4 C2", "J0 F7 C4 A6",
    "E2 B6 E4 K0", "J2 C6 J4 E6", "K2 K4 J6",
)


def shift(value, axis, distance):
    size = SIZES[axis]
    return lax.ppermute(value, axis, [(i, (i + distance) % size) for i in range(size)])


def meet(value, axis, masks, name):
    pairs = [(c * 4 + i, c * 4 + (i ^ masks[c])) for c in range(2) for i in range(4)]
    with jax.named_scope(name):
        return lax.ppermute(value, ("c", axis), pairs)


class Chain:
    def __init__(self):
        self.last = None

    def __call__(self, body, outs, ins, smem=(), scratch=()):
        extra = [] if self.last is None else [self.last]
        vmem = pl.BlockSpec(memory_space=pltpu.VMEM)
        count_in, count_out = len(smem) + len(ins), len(outs)

        def run(*refs):
            body(*refs[:count_in], *refs[count_in + len(extra):])

        result = pl.pallas_call(
            run,
            out_shape=tuple(jax.ShapeDtypeStruct(*o) for o in outs),
            in_specs=[pl.BlockSpec(memory_space=pltpu.SMEM)] * len(smem)
            + [vmem] * len(ins)
            + [pl.BlockSpec(memory_space=pl.ANY)] * len(extra),
            out_specs=(vmem,) * count_out,
            scratch_shapes=list(scratch),
            compiler_params=pltpu.CompilerParams(vmem_limit_bytes=VMEM_LIMIT),
            cost_estimate=pl.CostEstimate(flops=1, bytes_accessed=1, transcendentals=0),
        )(*smem, *ins, *extra)
        self.last = min(result, key=lambda a: a.size)
        return result


def pack_body(a_ref, b_ref, out_ref):
    width = a_ref.shape[1]
    out_ref[:, :width] = a_ref[...]
    out_ref[:, width:] = b_ref[...]


def stack_body(a_ref, b_ref, out_ref):
    rows = a_ref.shape[0]
    out_ref[:rows] = a_ref[...]
    out_ref[rows:] = b_ref[...]


def weights_body(gc, gb, uc, ub, dc, db, hist, wg_ref, wu_ref, wd_ref, wdt_ref):
    for k, (codes, blocks, out_ref) in enumerate(
        ((gc, gb, wg_ref), (uc, ub, wu_ref), (dc, db, wd_ref))
    ):
        scale = jnp.max(hist[k:k + 1, :], axis=1, keepdims=True) / CODE_LIMIT
        for b in range(blocks.shape[0]):
            part = codes[b * 128:(b + 1) * 128, :].astype(F32) * blocks[b:b + 1, :] * scale
            out_ref[b * 128:(b + 1) * 128, :] = part.astype(BF16)
            if k == 2:
                wdt_ref[:, b * 128:(b + 1) * 128] = part.T.astype(BF16)


def front_body(perm, src_ref, wg_ref, wu_ref, wd_ref, send_ref, keep_ref, rows_ref):
    half = send_ref.shape[0]
    quarter = half // 2
    for t in range(4):
        start = pl.multiple_of(perm[t] * quarter, quarter)
        rows_ref[t * quarter:(t + 1) * quarter, :] = src_ref[pl.ds(start, quarter), :]
    depth, width = wg_ref.shape
    for place, (first, w_ref) in enumerate(((0, wg_ref), (0, wu_ref), (depth, wd_ref))):
        left = rows_ref[:, first:first + depth]
        product = jnp.dot(left, w_ref[...], preferred_element_type=F32).astype(BF16)
        columns = slice(place * width, (place + 1) * width)
        keep_ref[:, columns] = product[:half]
        send_ref[:, columns] = product[half:]


def halve_body(*refs):
    count = (len(refs) - 2) // 2
    send_ref, left_ref = refs[-2:]
    half = refs[0].shape[0] // 2
    for i, (keep, got) in enumerate(zip(refs[:count], refs[count:])):
        total = (keep[...].astype(F32) + got[...].astype(F32)).astype(BF16)
        left_ref[i * half:(i + 1) * half] = total[:half]
        send_ref[i * half:(i + 1) * half] = total[half:]


def add_body(keep_ref, got_ref, out_ref):
    out_ref[...] = (keep_ref[...].astype(F32) + got_ref[...].astype(F32)).astype(BF16)


def middle_body(keep_ref, got_ref, out_ref):
    total = keep_ref[...].astype(F32) + got_ref[...].astype(F32)
    width = total.shape[1] // 3
    gate, up, back = total[:, :width], total[:, width:2 * width], total[:, 2 * width:]
    sig = jax.nn.sigmoid(gate)
    out_ref[:, :width] = (gate * sig * up).astype(BF16)
    out_ref[:, width:2 * width] = (back * up * sig * (1.0 + gate * (1.0 - sig))).astype(BF16)
    out_ref[:, 2 * width:] = (back * gate * sig).astype(BF16)


def unhalve_body(own_ref, got_ref, out_ref):
    half = own_ref.shape[0] // 2
    for i in range(2):
        out_ref[2 * i * half:(2 * i + 1) * half] = own_ref[i * half:(i + 1) * half]
        out_ref[(2 * i + 1) * half:(2 * i + 2) * half] = got_ref[i * half:(i + 1) * half]


def back_body(units, perm, near_ref, far_ref, w_ref, *outs):
    width = w_ref.shape[0]
    half = near_ref.shape[0] // units
    for part, ref in enumerate((near_ref, far_ref)):
        product = jnp.dot(ref[:, :width], w_ref[...], preferred_element_type=F32).astype(BF16)
        quarter = half // 2
        for i, out_ref in enumerate(outs):
            for t in range(2):
                start = pl.multiple_of(perm[2 * part + t] * quarter, quarter)
                place = i * half + t * quarter
                out_ref[pl.ds(start, quarter), :] = product[place:place + quarter]


def pile_body(*refs):
    place = 0
    for ref in refs[:-1]:
        refs[-1][place:place + ref.shape[0]] = ref[...]
        place += ref.shape[0]


def cores_body(got_ref, *refs):
    mine, (keep_ref, send_ref) = refs[:-2], refs[-2:]
    rows = mine[0].shape[0]
    half = rows // 2
    for i, ref in enumerate(mine):
        total = ref[...].astype(F32) + got_ref[i * rows:(i + 1) * rows].astype(F32)
        keep_ref[i * half:(i + 1) * half] = total[:half].astype(BF16)
        send_ref[i * half:(i + 1) * half] = total[half:].astype(BF16)


def pairs_body(keep_ref, got_ref, *outs):
    total = keep_ref[...].astype(F32) + got_ref[...].astype(F32)
    rows = outs[0].shape[0]
    for i, ref in enumerate(outs):
        ref[...] = total[i * rows:(i + 1) * rows].astype(BF16)


def total_body(*refs):
    total = refs[0][...].astype(F32)
    for ref in refs[1:-1]:
        total += ref[...].astype(F32)
    refs[-1][...] = total.astype(BF16)


def max_body(a_ref, b_ref, out_ref):
    out_ref[...] = jnp.maximum(a_ref[...], b_ref[...])


def contract(left, right):
    return lax.dot_general(left, right, (((0,), (0,)), ((), ())), preferred_element_type=F32)


def gather_rows(refs, columns, scratch):
    place = 0
    for ref in refs:
        scratch[place:place + ref.shape[0], :] = ref[:, columns]
        place += ref.shape[0]
    return scratch[...]


def gather_acts(refs, columns, scratch, rows_in_unit):
    place = 0
    half = rows_in_unit // 2
    for near, far in zip(refs[0::2], refs[1::2]):
        for i in range(near.shape[0] // half):
            for ref in (near, far):
                scratch[place:place + half, :] = ref[i * half:(i + 1) * half, columns]
                place += half
    return scratch[...]


def grad_body(which, depth, width, count, *refs):
    rows, acts, out_ref, left, right = refs[:count], refs[count:-3], refs[-3], refs[-2], refs[-1]
    places = [slice(width, 2 * width), slice(2 * width, 3 * width), slice(0, width)]
    first = slice(depth, 2 * depth) if which == 2 else slice(0, depth)
    r, a = gather_rows(rows, first, left), gather_acts(acts, places[which], right, rows[0].shape[0])
    out_ref[...] = contract(a, r) if which == 2 else contract(r, a)


def last_body(depth, width, count, act_count, hist, *refs):
    rows, refs = refs[:count], refs[count:]
    acts, totals, refs = refs[:act_count], refs[act_count:act_count + 3], refs[act_count + 3:]
    outs, peak_ref = refs[:3], refs[3]
    left, right = refs[-2:]
    places = [slice(width, 2 * width), slice(2 * width, 3 * width), slice(0, width)]
    x = gather_rows(rows, slice(0, depth), left)
    peak_ref[...] = jnp.zeros_like(peak_ref)
    for which in (0, 1, 2):
        if which == 2:
            x = gather_rows(rows, slice(depth, 2 * depth), left)
        a = gather_acts(acts, places[which], right, rows[0].shape[0])
        total = totals[which][...] + (contract(a, x) if which == 2 else contract(x, a))
        peak = jnp.max(jnp.max(jnp.abs(total), axis=0, keepdims=True), axis=1, keepdims=True)
        peak_ref[which:which + 1, :] = jnp.broadcast_to(peak, (1, peak_ref.shape[1]))
        scale = jnp.max(hist[which:which + 1, :], axis=1, keepdims=True)
        outs[which][...] = jnp.clip(total / scale, -1.0, 1.0).astype(BF16)


def shards(
    inputs,
    cotangent,
    gate_codes,
    gate_blocks,
    up_codes,
    up_blocks,
    down_codes,
    down_blocks,
    weight_history,
    grad_history,
):
    core, x = lax.axis_index("c"), lax.axis_index("x")
    first = jnp.where(core == 0, FIRST[0], FIRST[1])
    second = jnp.where(core == 0, SECOND[0], SECOND[1])
    perm_mine = jnp.stack([x, x ^ second, x ^ first, x ^ first ^ second]).astype(jnp.int32)
    perm_other = jnp.array([0, 2, 1, 3], jnp.int32)
    perm_same = jnp.arange(4, dtype=jnp.int32)
    depth, width = gate_codes.shape
    tokens = inputs.shape[0]
    rows_in_unit, half, quarter = 2 * tokens, tokens, tokens // 2

    call = Chain()
    (own,) = call(pack_body, [((tokens, 2 * depth), BF16)], [inputs, cotangent])
    own_zl = shift(own, "zl", 1)
    wg, wu, wd, wd_t = call(
        weights_body,
        [((depth, width), BF16), ((depth, width), BF16), ((width, depth), BF16), ((depth, width), BF16)],
        [gate_codes, gate_blocks, up_codes, up_blocks, down_codes, down_blocks, weight_history],
    )
    (pair,) = call(stack_body, [((rows_in_unit, 2 * depth), BF16)], [own, own_zl])
    here = {0: pair, 1: shift(pair, "y", -1), 3: shift(pair, "y", 1)}

    rows, keep, got, held, far, there, outs = {}, {}, {}, {}, {}, {}, {}
    wide = 3 * width
    chunk_rows = 2 * rows_in_unit

    def front(u):
        distance, mine = CHUNKS[u // 2], u % 2 == 0
        perm = (perm_same if distance == 2 else perm_mine) if mine else perm_other
        sent, keep[u], rows[u] = call(
            front_body,
            [((half, wide), BF16)] * 2 + [((rows_in_unit, 2 * depth), BF16)],
            [here[distance] if mine else there[distance], wg, wu, wd_t],
            smem=[perm],
        )
        got[u] = meet(sent, "x", FIRST, f"halves_{u}")
        if mine:
            with jax.named_scope(f"rows_{u}"):
                there[distance] = shift(rows[u], "c", 1)
        if distance == 1 and mine:
            with jax.named_scope("rows_far"):
                here[2] = shift(rows[u], "y", -1)

    def reduce_step(kind, u):
        count = 2 if MODES[u // 2] == "m" else 1
        units = range(u, u + count)
        if kind == "A":
            sent, keep[u] = call(
                halve_body,
                [((count * quarter, wide), BF16)] * 2,
                [keep[i] for i in units] + [got[i] for i in units],
            )
            got[u] = meet(sent, "x", SECOND, f"quarters_{u}")
        elif kind == "E":
            (keep[u],) = call(middle_body, [(keep[u].shape, BF16)], [keep[u], got[u]])
            got[u] = meet(keep[u], "x", SECOND, f"back_quarters_{u}")
        else:
            (keep[u],) = call(add_body, [(keep[u].shape, BF16)], [keep[u], got[u]])
            masks, name = (FIRST, "first") if kind == "B" else (SECOND, "second")
            got[u] = meet(keep[u], "zh", masks, f"rows_{name}_{u}")

    def gather_step(u):
        body, count = (unhalve_body, 2) if MODES[u // 2] == "m" else (pile_body, 1)
        (held[u],) = call(body, [((count * half, wide), BF16)], [keep[u], got[u]])
        far[u] = meet(held[u], "x", FIRST, f"back_halves_{u}")

    def finish(u):
        count = 2 if MODES[u // 2] == "m" else 1
        came_back = call(
            functools.partial(back_body, count),
            [((rows_in_unit, depth), BF16)] * count,
            [held[u], far[u], wd],
            smem=[perm_mine],
        )
        for i, value in enumerate(came_back):
            outs[u + i] = value

    def starts(chunks):
        return [u for p in chunks for u in ((2 * p,) if MODES[p] == "m" else (2 * p, 2 * p + 1))]

    for step in " ".join(ORDER).split():
        kind, u = step[0], int(step[1:])
        if kind == "F":
            front(u)
        elif kind in "ABCE":
            reduce_step(kind, u)
        elif kind == "J":
            gather_step(u)
        else:
            finish(u)

    def send_cores(chunks):
        other = [outs[2 * p + 1] for p in chunks]
        if len(other) > 1:
            other = call(pile_body, [((len(other) * rows_in_unit, depth), BF16)], other)
        return shift(other[0], "c", 1), [outs[2 * p] for p in chunks], [CHUNKS[p] for p in chunks]

    def send_pairs(came, mine):
        left, sent = call(cores_body, [((len(mine) * half, depth), BF16)] * 2, [came] + mine)
        return left, shift(sent, "zl", 1)

    def send_home(left, came, distances):
        blocks = call(pairs_body, [((half, depth), BF16)] * len(distances), [left, came])
        return [shift(b, "y", d) if d else b for b, d in zip(blocks, distances)]

    early, late = range(EARLY), range(EARLY, len(CHUNKS))
    came, mine, distances = send_cores(early)
    early_rows = [rows[u] for p in early for u in (2 * p, 2 * p + 1)]
    early_acts = [part for u in starts(early) for part in (held[u], far[u])]
    totals = []
    for which in range(3):
        (total,) = call(
            functools.partial(grad_body, which, depth, width, len(early_rows)),
            [((width, depth) if which == 2 else (depth, width), F32)],
            early_rows + early_acts,
            scratch=[
                pltpu.VMEM((EARLY * chunk_rows, depth), BF16),
                pltpu.VMEM((EARLY * chunk_rows, width), BF16),
            ],
        )
        totals.append(total)
        if which == 0:
            left, came = send_pairs(came, mine)
    blocks = send_home(left, came, distances)
    late_rows = [rows[u] for p in late for u in (2 * p, 2 * p + 1)]
    late_acts = [part for u in starts(late) for part in (held[u], far[u])]
    grad_gate, grad_up, grad_down, peaks = call(
        functools.partial(last_body, depth, width, len(late_rows), len(late_acts)),
        [((depth, width), BF16), ((depth, width), BF16), ((width, depth), BF16), ((8, 128), F32)],
        [grad_history] + late_rows + late_acts + totals,
        scratch=[
            pltpu.VMEM((len(late) * chunk_rows, depth), BF16),
            pltpu.VMEM((len(late) * chunk_rows, width), BF16),
        ],
    )
    steps = [("c", 1), ("zl", 1), ("y", 1), ("y", 3), ("zh", 1), ("zh", 3), ("x", 1), ("x", 3)]
    for i, (axis, mask) in enumerate(steps):
        size = SIZES[axis]
        seen = lax.ppermute(peaks, axis, [(j, j ^ mask) for j in range(size)])
        if i == 0:
            for u in starts(late):
                finish(u)
            came, mine, distances = send_cores(late)
        elif i == 1:
            left, came = send_pairs(came, mine)
        elif i == 2:
            blocks += send_home(left, came, distances)
        elif i == 6:
            (block_output,) = call(total_body, [((half, depth), BF16)], blocks)
        (peaks,) = call(max_body, [((8, 128), F32)], [peaks, seen])
    peak_all = peaks[:3, 0]
    return (block_output, grad_gate, grad_up, grad_down, peak_all)


def solution(mesh):
    names = ("y", "zl", "c", "x", "zh")
    fine = Mesh(mesh.devices.reshape([SIZES[n] for n in names]), names)
    node, local = ("y", "zl", "c"), ("x", "zh")
    acts, weights, weights_t = P(node, local), P(local, node), P(node, local)
    return jax.shard_map(
        shards,
        mesh=fine,
        in_specs=(acts, acts) + (weights,) * 4 + (weights_t,) * 2 + (P(), P()),
        out_specs=(acts, weights, weights, weights_t, P()),
        check_vma=False,
    )
```

```python
import functools

import jax
import jax.numpy as jnp
from jax import lax
from jax.experimental import pallas as pl
from jax.experimental.pallas import tpu as pltpu
from jax.sharding import Mesh, PartitionSpec as P

CODE_LIMIT = 448.0
SIZES = {"y": 4, "zl": 2, "c": 2, "x": 4, "zh": 4}
VMEM_LIMIT = 40 * 1024 * 1024
F32, BF16 = jnp.float32, jnp.bfloat16
CHUNKS = (0, 1, 3, 2)
MODES = "mmmm"
EARLY = 3
FIRST, SECOND = (1, 3), (3, 1)
ORDER = (
    "F0 F1 A0 F2", "F3 B0 F4 A2", "F5 C0 B2 A4", "E0 F6 B4 C2", "J0 F7 C4 A6",
    "E2 B6 E4 K0", "J2 C6 J4 E6", "K2 J6 K4",
)


def shift(value, axis, distance):
    size = SIZES[axis]
    return lax.ppermute(value, axis, [(i, (i + distance) % size) for i in range(size)])


def meet(value, axis, masks, name):
    pairs = [(c * 4 + i, c * 4 + (i ^ masks[c])) for c in range(2) for i in range(4)]
    with jax.named_scope(name):
        return lax.ppermute(value, ("c", axis), pairs)


class Chain:
    def __init__(self):
        self.last = None

    def __call__(self, body, outs, ins, smem=(), scratch=()):
        extra = [] if self.last is None else [self.last]
        vmem = pl.BlockSpec(memory_space=pltpu.VMEM)
        count_in, count_out = len(smem) + len(ins), len(outs)

        def run(*refs):
            body(*refs[:count_in], *refs[count_in + len(extra):])

        result = pl.pallas_call(
            run,
            out_shape=tuple(jax.ShapeDtypeStruct(*o) for o in outs),
            in_specs=[pl.BlockSpec(memory_space=pltpu.SMEM)] * len(smem)
            + [vmem] * len(ins)
            + [pl.BlockSpec(memory_space=pl.ANY)] * len(extra),
            out_specs=(vmem,) * count_out,
            scratch_shapes=list(scratch),
            compiler_params=pltpu.CompilerParams(vmem_limit_bytes=VMEM_LIMIT),
            cost_estimate=pl.CostEstimate(flops=1, bytes_accessed=1, transcendentals=0),
        )(*smem, *ins, *extra)
        self.last = min(result, key=lambda a: a.size)
        return result


def pack_body(a_ref, b_ref, out_ref):
    width = a_ref.shape[1]
    out_ref[:, :width] = a_ref[...]
    out_ref[:, width:] = b_ref[...]


def stack_body(a_ref, b_ref, out_ref):
    rows = a_ref.shape[0]
    out_ref[:rows] = a_ref[...]
    out_ref[rows:] = b_ref[...]


def weights_body(gc, gb, uc, ub, dc, db, hist, wg_ref, wu_ref, wd_ref, wdt_ref):
    for k, (codes, blocks, out_ref) in enumerate(
        ((gc, gb, wg_ref), (uc, ub, wu_ref), (dc, db, wd_ref))
    ):
        scale = jnp.max(hist[k:k + 1, :], axis=1, keepdims=True) / CODE_LIMIT
        for b in range(blocks.shape[0]):
            part = codes[b * 128:(b + 1) * 128, :].astype(F32) * blocks[b:b + 1, :] * scale
            out_ref[b * 128:(b + 1) * 128, :] = part.astype(BF16)
            if k == 2:
                wdt_ref[:, b * 128:(b + 1) * 128] = part.T.astype(BF16)


def front_body(perm, src_ref, wg_ref, wu_ref, wd_ref, send_ref, keep_ref, rows_ref):
    half = send_ref.shape[0]
    quarter = half // 2
    for t in range(4):
        start = pl.multiple_of(perm[t] * quarter, quarter)
        rows_ref[t * quarter:(t + 1) * quarter, :] = src_ref[pl.ds(start, quarter), :]
    depth, width = wg_ref.shape
    for place, (first, w_ref) in enumerate(((0, wg_ref), (0, wu_ref), (depth, wd_ref))):
        left = rows_ref[:, first:first + depth]
        product = jnp.dot(left, w_ref[...], preferred_element_type=F32).astype(BF16)
        columns = slice(place * width, (place + 1) * width)
        keep_ref[:, columns] = product[:half]
        send_ref[:, columns] = product[half:]


def halve_body(*refs):
    count = (len(refs) - 2) // 2
    send_ref, left_ref = refs[-2:]
    half = refs[0].shape[0] // 2
    for i, (keep, got) in enumerate(zip(refs[:count], refs[count:])):
        total = (keep[...].astype(F32) + got[...].astype(F32)).astype(BF16)
        left_ref[i * half:(i + 1) * half] = total[:half]
        send_ref[i * half:(i + 1) * half] = total[half:]


def add_body(keep_ref, got_ref, out_ref):
    out_ref[...] = (keep_ref[...].astype(F32) + got_ref[...].astype(F32)).astype(BF16)


def middle_body(keep_ref, got_ref, out_ref):
    total = keep_ref[...].astype(F32) + got_ref[...].astype(F32)
    width = total.shape[1] // 3
    gate, up, back = total[:, :width], total[:, width:2 * width], total[:, 2 * width:]
    sig = jax.nn.sigmoid(gate)
    out_ref[:, :width] = (gate * sig * up).astype(BF16)
    out_ref[:, width:2 * width] = (back * up * sig * (1.0 + gate * (1.0 - sig))).astype(BF16)
    out_ref[:, 2 * width:] = (back * gate * sig).astype(BF16)


def unhalve_body(own_ref, got_ref, out_ref):
    half = own_ref.shape[0] // 2
    for i in range(2):
        out_ref[2 * i * half:(2 * i + 1) * half] = own_ref[i * half:(i + 1) * half]
        out_ref[(2 * i + 1) * half:(2 * i + 2) * half] = got_ref[i * half:(i + 1) * half]


def back_body(units, perm, near_ref, far_ref, w_ref, *outs):
    width = w_ref.shape[0]
    half = near_ref.shape[0] // units
    for part, ref in enumerate((near_ref, far_ref)):
        product = jnp.dot(ref[:, :width], w_ref[...], preferred_element_type=F32).astype(BF16)
        quarter = half // 2
        for i, out_ref in enumerate(outs):
            for t in range(2):
                start = pl.multiple_of(perm[2 * part + t] * quarter, quarter)
                place = i * half + t * quarter
                out_ref[pl.ds(start, quarter), :] = product[place:place + quarter]


def pile_body(*refs):
    place = 0
    for ref in refs[:-1]:
        refs[-1][place:place + ref.shape[0]] = ref[...]
        place += ref.shape[0]


def cores_body(got_ref, *refs):
    mine, (keep_ref, send_ref) = refs[:-2], refs[-2:]
    rows = mine[0].shape[0]
    half = rows // 2
    for i, ref in enumerate(mine):
        total = ref[...].astype(F32) + got_ref[i * rows:(i + 1) * rows].astype(F32)
        keep_ref[i * half:(i + 1) * half] = total[:half].astype(BF16)
        send_ref[i * half:(i + 1) * half] = total[half:].astype(BF16)


def pairs_body(keep_ref, got_ref, *outs):
    total = keep_ref[...].astype(F32) + got_ref[...].astype(F32)
    rows = outs[0].shape[0]
    for i, ref in enumerate(outs):
        ref[...] = total[i * rows:(i + 1) * rows].astype(BF16)


def total_body(*refs):
    total = refs[0][...].astype(F32)
    for ref in refs[1:-1]:
        total += ref[...].astype(F32)
    refs[-1][...] = total.astype(BF16)


def max_body(a_ref, b_ref, out_ref):
    out_ref[...] = jnp.maximum(a_ref[...], b_ref[...])


def contract(left, right):
    return lax.dot_general(left, right, (((0,), (0,)), ((), ())), preferred_element_type=F32)


def gather_rows(refs, columns, scratch):
    place = 0
    for ref in refs:
        scratch[place:place + ref.shape[0], :] = ref[:, columns]
        place += ref.shape[0]
    return scratch[...]


def gather_acts(refs, columns, scratch, rows_in_unit):
    place = 0
    half = rows_in_unit // 2
    for near, far in zip(refs[0::2], refs[1::2]):
        for i in range(near.shape[0] // half):
            for ref in (near, far):
                scratch[place:place + half, :] = ref[i * half:(i + 1) * half, columns]
                place += half
    return scratch[...]


def grad_body(which, depth, width, count, *refs):
    rows, acts, out_ref, left, right = refs[:count], refs[count:-3], refs[-3], refs[-2], refs[-1]
    places = [slice(width, 2 * width), slice(2 * width, 3 * width), slice(0, width)]
    first = slice(depth, 2 * depth) if which == 2 else slice(0, depth)
    r, a = gather_rows(rows, first, left), gather_acts(acts, places[which], right, rows[0].shape[0])
    out_ref[...] = contract(a, r) if which == 2 else contract(r, a)


def last_body(depth, width, count, act_count, hist, *refs):
    rows, refs = refs[:count], refs[count:]
    acts, totals, refs = refs[:act_count], refs[act_count:act_count + 3], refs[act_count + 3:]
    outs, peak_ref = refs[:3], refs[3]
    left, right = refs[-2:]
    places = [slice(width, 2 * width), slice(2 * width, 3 * width), slice(0, width)]
    x = gather_rows(rows, slice(0, depth), left)
    peak_ref[...] = jnp.zeros_like(peak_ref)
    for which in (0, 1, 2):
        if which == 2:
            x = gather_rows(rows, slice(depth, 2 * depth), left)
        a = gather_acts(acts, places[which], right, rows[0].shape[0])
        total = totals[which][...] + (contract(a, x) if which == 2 else contract(x, a))
        peak = jnp.max(jnp.max(jnp.abs(total), axis=0, keepdims=True), axis=1, keepdims=True)
        peak_ref[which:which + 1, :] = jnp.broadcast_to(peak, (1, peak_ref.shape[1]))
        scale = jnp.max(hist[which:which + 1, :], axis=1, keepdims=True)
        outs[which][...] = jnp.clip(total / scale, -1.0, 1.0).astype(BF16)


def shards(
    inputs,
    cotangent,
    gate_codes,
    gate_blocks,
    up_codes,
    up_blocks,
    down_codes,
    down_blocks,
    weight_history,
    grad_history,
):
    core, x = lax.axis_index("c"), lax.axis_index("x")
    first = jnp.where(core == 0, FIRST[0], FIRST[1])
    second = jnp.where(core == 0, SECOND[0], SECOND[1])
    perm_mine = jnp.stack([x, x ^ second, x ^ first, x ^ first ^ second]).astype(jnp.int32)
    perm_other = jnp.array([0, 2, 1, 3], jnp.int32)
    perm_same = jnp.arange(4, dtype=jnp.int32)
    depth, width = gate_codes.shape
    tokens = inputs.shape[0]
    rows_in_unit, half, quarter = 2 * tokens, tokens, tokens // 2

    call = Chain()
    (own,) = call(pack_body, [((tokens, 2 * depth), BF16)], [inputs, cotangent])
    own_zl = shift(own, "zl", 1)
    wg, wu, wd, wd_t = call(
        weights_body,
        [((depth, width), BF16), ((depth, width), BF16), ((width, depth), BF16), ((depth, width), BF16)],
        [gate_codes, gate_blocks, up_codes, up_blocks, down_codes, down_blocks, weight_history],
    )
    (pair,) = call(stack_body, [((rows_in_unit, 2 * depth), BF16)], [own, own_zl])
    here = {0: pair, 1: shift(pair, "y", -1), 3: shift(pair, "y", 1)}

    rows, keep, got, held, far, there, outs = {}, {}, {}, {}, {}, {}, {}
    wide = 3 * width
    chunk_rows = 2 * rows_in_unit

    def front(u):
        distance, mine = CHUNKS[u // 2], u % 2 == 0
        perm = (perm_same if distance == 2 else perm_mine) if mine else perm_other
        sent, keep[u], rows[u] = call(
            front_body,
            [((half, wide), BF16)] * 2 + [((rows_in_unit, 2 * depth), BF16)],
            [here[distance] if mine else there[distance], wg, wu, wd_t],
            smem=[perm],
        )
        got[u] = meet(sent, "x", FIRST, f"halves_{u}")
        if mine:
            with jax.named_scope(f"rows_{u}"):
                there[distance] = shift(rows[u], "c", 1)
        if distance == 1 and mine:
            with jax.named_scope("rows_far"):
                here[2] = shift(rows[u], "y", -1)

    def reduce_step(kind, u):
        count = 2 if MODES[u // 2] == "m" else 1
        units = range(u, u + count)
        if kind == "A":
            sent, keep[u] = call(
                halve_body,
                [((count * quarter, wide), BF16)] * 2,
                [keep[i] for i in units] + [got[i] for i in units],
            )
            got[u] = meet(sent, "x", SECOND, f"quarters_{u}")
        elif kind == "E":
            (keep[u],) = call(middle_body, [(keep[u].shape, BF16)], [keep[u], got[u]])
            got[u] = meet(keep[u], "x", SECOND, f"back_quarters_{u}")
        else:
            (keep[u],) = call(add_body, [(keep[u].shape, BF16)], [keep[u], got[u]])
            masks, name = (FIRST, "first") if kind == "B" else (SECOND, "second")
            got[u] = meet(keep[u], "zh", masks, f"rows_{name}_{u}")

    def gather_step(u):
        body, count = (unhalve_body, 2) if MODES[u // 2] == "m" else (pile_body, 1)
        (held[u],) = call(body, [((count * half, wide), BF16)], [keep[u], got[u]])
        far[u] = meet(held[u], "x", FIRST, f"back_halves_{u}")

    def finish(u):
        count = 2 if MODES[u // 2] == "m" else 1
        came_back = call(
            functools.partial(back_body, count),
            [((rows_in_unit, depth), BF16)] * count,
            [held[u], far[u], wd],
            smem=[perm_mine],
        )
        for i, value in enumerate(came_back):
            outs[u + i] = value

    def starts(chunks):
        return [u for p in chunks for u in ((2 * p,) if MODES[p] == "m" else (2 * p, 2 * p + 1))]

    for step in " ".join(ORDER).split():
        kind, u = step[0], int(step[1:])
        if kind == "F":
            front(u)
        elif kind in "ABCE":
            reduce_step(kind, u)
        elif kind == "J":
            gather_step(u)
        else:
            finish(u)

    def send_cores(chunks):
        other = [outs[2 * p + 1] for p in chunks]
        if len(other) > 1:
            other = call(pile_body, [((len(other) * rows_in_unit, depth), BF16)], other)
        return shift(other[0], "c", 1), [outs[2 * p] for p in chunks], [CHUNKS[p] for p in chunks]

    def send_pairs(came, mine):
        left, sent = call(cores_body, [((len(mine) * half, depth), BF16)] * 2, [came] + mine)
        return left, shift(sent, "zl", 1)

    def send_home(left, came, distances):
        blocks = call(pairs_body, [((half, depth), BF16)] * len(distances), [left, came])
        return [shift(b, "y", d) if d else b for b, d in zip(blocks, distances)]

    early, late = range(EARLY), range(EARLY, len(CHUNKS))
    came, mine, distances = send_cores(early)
    early_rows = [rows[u] for p in early for u in (2 * p, 2 * p + 1)]
    early_acts = [part for u in starts(early) for part in (held[u], far[u])]
    totals = []
    for which in range(3):
        (total,) = call(
            functools.partial(grad_body, which, depth, width, len(early_rows)),
            [((width, depth) if which == 2 else (depth, width), F32)],
            early_rows + early_acts,
            scratch=[
                pltpu.VMEM((EARLY * chunk_rows, depth), BF16),
                pltpu.VMEM((EARLY * chunk_rows, width), BF16),
            ],
        )
        totals.append(total)
        if which == 0:
            left, came = send_pairs(came, mine)
    blocks = send_home(left, came, distances)
    late_rows = [rows[u] for p in late for u in (2 * p, 2 * p + 1)]
    for u in starts(late):
        finish(u)
    came, mine, distances = send_cores(late)
    late_acts = [part for u in starts(late) for part in (held[u], far[u])]
    grad_gate, grad_up, grad_down, peaks = call(
        functools.partial(last_body, depth, width, len(late_rows), len(late_acts)),
        [((depth, width), BF16), ((depth, width), BF16), ((width, depth), BF16), ((8, 128), F32)],
        [grad_history] + late_rows + late_acts + totals,
        scratch=[
            pltpu.VMEM((len(late) * chunk_rows, depth), BF16),
            pltpu.VMEM((len(late) * chunk_rows, width), BF16),
        ],
    )
    steps = [("c", 1), ("zl", 1), ("y", 1), ("y", 3), ("zh", 1), ("zh", 3), ("x", 1), ("x", 3)]
    for i, (axis, mask) in enumerate(steps):
        size = SIZES[axis]
        seen = lax.ppermute(peaks, axis, [(j, j ^ mask) for j in range(size)])
        if i == 0:
            left, came = send_pairs(came, mine)
        elif i == 1:
            blocks += send_home(left, came, distances)
        elif i == 5:
            (block_output,) = call(total_body, [((half, depth), BF16)], blocks)
        (peaks,) = call(max_body, [((8, 128), F32)], [peaks, seen])
    peak_all = peaks[:3, 0]
    return (block_output, grad_gate, grad_up, grad_down, peak_all)


def solution(mesh):
    names = ("y", "zl", "c", "x", "zh")
    fine = Mesh(mesh.devices.reshape([SIZES[n] for n in names]), names)
    node, local = ("y", "zl", "c"), ("x", "zh")
    acts, weights, weights_t = P(node, local), P(local, node), P(node, local)
    return jax.shard_map(
        shards,
        mesh=fine,
        in_specs=(acts, acts) + (weights,) * 4 + (weights_t,) * 2 + (P(), P()),
        out_specs=(acts, weights, weights, weights_t, P()),
        check_vma=False,
    )
```
